256 devices in a mesh: ctx: 32 (over z_hi, x, y), ch: 8 (over z_lo, core).
Axes of the slice: x: 4, y: 4, z: 8 (z_hi: 2, z_lo: 4; z = z_hi * 4 + z_lo), core: 2. Of those that a mesh axis runs over, the one named last changes fastest.
Arguments:
- query_proj: float32 [8192, 4096], P('ctx', 'ch'), may hold values from -6 to 6
- key_proj: float32 [8192, 4096], P('ctx', 'ch'), may hold values from -6 to 6
- value_proj: float32 [8192, 4096], P('ctx', 'ch'), may hold values from -6 to 6
- filter_taps: float32 [8192, 4096], P('ctx', 'ch'), may hold values from -0.0625 to 0.0625
- cotangent: float32 [8192, 4096], P('ctx', 'ch'), may hold values from -0.625 to 0.625
Outputs:
- output: float32 [8192, 4096], P('ctx', 'ch')
- grad_query: float32 [8192, 4096], P('ctx', 'ch')
- grad_key: float32 [8192, 4096], P('ctx', 'ch')
- grad_value: float32 [8192, 4096], P('ctx', 'ch')
- grad_filter: float32 [8192, 4096], P('ctx', 'ch')
The draws below stay inside these ranges and needn't reach their ends.
All inputs are finite; a program needn't handle non-finite values.
Results may differ from the reference program's by a relative error of at most 0.0001.
Values sent between devices are 32-bit elements; how exact they have to be, the bound alone decides.
A program may use at most 128 MiB of HBM per device.

```python
import jax
import jax.numpy as jnp
from jax import lax

CHANNELS = 4096
LENGTH = 8192


def level_of(own_key, shape, pieces, least, high):
    gain, own = 1.0, jax.random.fold_in(own_key, 6)
    for position, blocks in pieces:
        steps = jnp.exp(jax.random.uniform(jax.random.fold_in(own, position), (blocks,), jnp.float32, least / len(pieces), high / len(pieces)))
        gain = gain * jnp.repeat(steps, shape[position] // blocks).reshape([-1 if axis == position else 1 for axis in range(len(shape))])
    return gain


def gaussian(own_key, extent, spread, limit, cuts=(), dtype=jnp.bfloat16):
    drawn = jax.random.normal(own_key, extent, jnp.float32) * spread
    if len(cuts) > 0:
        drawn = level_of(own_key, extent, cuts, -0.22, 0.18) * drawn
    return jnp.clip(drawn, min=-limit, max=limit).astype(dtype)


def setup_inputs(seed: int = 0) -> dict:
    key_list = jax.random.split(jax.random.key(seed), 6)
    return {
        "query_proj": gaussian(key_list[0], (LENGTH, CHANNELS), 1.0, 6.0, ((0, 32), (1, 8)), jnp.float32),
        "key_proj": gaussian(key_list[1], (LENGTH, CHANNELS), 1.0, 6.0, ((0, 32), (1, 8)), jnp.float32),
        "value_proj": gaussian(key_list[2], (LENGTH, CHANNELS), 1.0, 6.0, ((0, 32), (1, 8)), jnp.float32),
        "filter_taps": gaussian(key_list[3], (LENGTH, CHANNELS), LENGTH ** -0.5, 0.0625, ((0, 32), (1, 8)), jnp.float32),
        "cotangent": gaussian(key_list[4], (LENGTH, CHANNELS), (LENGTH ** -0.25), 0.625, ((0, 32), (1, 8)), jnp.float32),
    }


def reference(query_proj, key_proj, value_proj, filter_taps, cotangent):
    seq_len = query_proj.shape[0]
    padded_len = 2 * seq_len
    block_width = min(512, CHANNELS)
    group_count = CHANNELS // block_width

    def split_up(array):
        return array.reshape(seq_len, group_count, block_width).transpose(1, 0, 2)

    def join_back(array):
        return array.transpose(1, 0, 2).reshape(seq_len, CHANNELS).astype(jnp.float32)

    def one_group(operands):
        query_blk, key_blk, value_blk, taps_blk, cot_blk = operands
        mixed_in = key_blk * value_blk
        mixed_spec = jnp.fft.rfft(mixed_in, n=padded_len, axis=0)
        taps_spec = jnp.fft.rfft(taps_blk, n=padded_len, axis=0)
        convolved = jnp.fft.irfft(mixed_spec * taps_spec, n=padded_len, axis=0)[:seq_len]
        upstream = cot_blk * query_blk
        up_spec = jnp.fft.rfft(upstream, n=padded_len, axis=0)
        grad_mixed = jnp.fft.irfft(jnp.conj(taps_spec) * up_spec, n=padded_len, axis=0)[:seq_len]
        grad_taps = jnp.fft.irfft(jnp.conj(mixed_spec) * up_spec, n=padded_len, axis=0)[:seq_len]
        return (query_blk * convolved, cot_blk * convolved, grad_mixed * value_blk,
                grad_mixed * key_blk, grad_taps)

    operands = (split_up(query_proj), split_up(key_proj), split_up(value_proj),
                split_up(filter_taps), split_up(cotangent))
    results = lax.map(one_group, operands)
    return (join_back(results[0]), join_back(results[1]), join_back(results[2]),
            join_back(results[3]), join_back(results[4]))
```

```python
import functools
import math

import jax
import jax.numpy as jnp
import ml_dtypes
import numpy as np
from jax import lax
from jax.experimental import pallas as pl
from jax.experimental.pallas import tpu as pltpu
from jax.sharding import PartitionSpec as P

MESH = pl.DeviceIdType.MESH
BF16 = jnp.bfloat16
F32 = jnp.float32

BLOCKS = 32
ROW = 256
CHUNK = 8
CHUNKS = 2
SIDE = BLOCKS * CHUNK
PADDED = 2 * BLOCKS * ROW

PLANE = (
    (0, 1), (3, 0), (0, 3), (1, 0), (1, 1), (3, 3), (1, 3), (3, 1),
    (0, 2), (2, 0), (2, 1), (1, 2), (2, 3), (3, 2), (2, 2),
)
OFFSETS = ((1, 0, 0),) + tuple(o for dx, dy in PLANE for o in ((0, dx, dy), (1, dx, dy)))
PEERS = len(OFFSETS)


def split_np(values):
    high = values.astype(ml_dtypes.bfloat16)
    low = (values - high.astype(np.float64)).astype(ml_dtypes.bfloat16)
    return high, low


@functools.lru_cache(maxsize=None)
def tables():
    two_pi = 2.0 * math.pi
    half = np.arange(BLOCKS) + 0.5
    block = np.arange(BLOCKS)
    row = np.arange(ROW)
    eye = np.eye(CHUNK)
    psi = two_pi * np.outer(half, block) / (2 * BLOCKS)
    outer = np.concatenate([np.kron(np.cos(psi), eye), np.kron(-np.sin(psi), eye)], axis=0)
    high, low = split_np(outer)
    outer3 = np.concatenate([high, low, high], axis=1)
    theta = two_pi * np.outer(half, row) / PADDED
    turn_re = np.repeat(np.cos(theta), CHUNK, axis=0).astype(np.float32)
    turn_im = np.repeat(-np.sin(theta), CHUNK, axis=0).astype(np.float32)
    phi = two_pi * (np.outer(row, row) % ROW) / ROW
    inner = np.block([[np.cos(phi), -np.sin(phi)], [np.sin(phi), np.cos(phi)]])
    high, low = split_np(inner)
    inner3 = np.concatenate([high, high, low], axis=0)
    back = np.concatenate([np.kron(np.cos(psi.T), eye), np.kron(np.sin(psi.T), eye)], axis=1)
    high, low = split_np(back * (2.0 / PADDED))
    back3 = np.concatenate([high, low, high], axis=1)
    return outer3, turn_re, turn_im, inner3, back3


def halves(values):
    high = values.astype(BF16)
    return high, (values - high.astype(F32)).astype(BF16)


def transform(arrived, results, outer3, turn_re, turn_im, inner3, back3, wide):
    t_re = turn_re[...]
    t_im = turn_im[...]
    for sig in range(3):
        high, low = halves(arrived[:, sig].reshape(SIDE, ROW))
        mixed = jnp.dot(
            outer3[...], jnp.concatenate([high, high, low], axis=0), preferred_element_type=F32
        )
        z_re, z_im = mixed[:SIDE], mixed[SIDE:]
        rows = pl.ds(sig * SIDE, SIDE)
        high, low = halves(z_re * t_re - z_im * t_im)
        wide[rows, 0 * ROW : 1 * ROW] = high
        wide[rows, 2 * ROW : 3 * ROW] = low
        wide[rows, 4 * ROW : 5 * ROW] = high
        high, low = halves(z_re * t_im + z_im * t_re)
        wide[rows, 1 * ROW : 2 * ROW] = high
        wide[rows, 3 * ROW : 4 * ROW] = low
        wide[rows, 5 * ROW : 6 * ROW] = high
    spec = jnp.dot(wide[...], inner3[...], preferred_element_type=F32)
    m_re, m_im = spec[:SIDE, :ROW], spec[:SIDE, ROW:]
    h_re, h_im = spec[SIDE : 2 * SIDE, :ROW], spec[SIDE : 2 * SIDE, ROW:]
    u_re, u_im = spec[2 * SIDE :, :ROW], spec[2 * SIDE :, ROW:]
    products = (
        (m_re * h_re - m_im * h_im, -(m_re * h_im + m_im * h_re)),
        (h_re * u_re + h_im * u_im, h_im * u_re - h_re * u_im),
        (m_re * u_re + m_im * u_im, m_im * u_re - m_re * u_im),
    )
    for sig, (p_re, p_im) in enumerate(products):
        rows = pl.ds(sig * SIDE, SIDE)
        high, low = halves(p_re)
        wide[rows, 0 * ROW : 1 * ROW] = high
        wide[rows, 2 * ROW : 3 * ROW] = low
        wide[rows, 4 * ROW : 5 * ROW] = high
        high, low = halves(p_im)
        wide[rows, 1 * ROW : 2 * ROW] = high
        wide[rows, 3 * ROW : 4 * ROW] = low
        wide[rows, 5 * ROW : 6 * ROW] = high
    inv = jnp.dot(wide[...], inner3[...], preferred_element_type=F32)
    for sig in range(3):
        v_re = inv[sig * SIDE : (sig + 1) * SIDE, :ROW]
        v_im = inv[sig * SIDE : (sig + 1) * SIDE, ROW:]
        re_high, re_low = halves(v_re * t_re - v_im * t_im)
        im_high, im_low = halves(v_re * t_im + v_im * t_re)
        stacked = jnp.concatenate([re_high, im_high, re_high, im_high, re_low, im_low], axis=0)
        out = jnp.dot(back3[...], stacked, preferred_element_type=F32)
        results[:, sig] = out.reshape(BLOCKS, CHUNK, ROW)


def exchange_kernel(
    q_ref, k_ref, v_ref, f_ref, g_ref, outer_hbm, re_hbm, im_hbm, inner_hbm, back_hbm,
    returned,
    outgoing, arrived, results, wide, outer3, turn_re, turn_im, inner3, back3,
    table_sem, go_send, go_recv, back_send, back_recv, own_sem,
):
    ctx = lax.axis_index("ctx")
    ch = lax.axis_index("ch")
    z_hi = ctx // 16
    x = lax.rem(ctx // 4, 4)
    y = lax.rem(ctx, 4)
    peers = [
        lax.rem(z_hi + dz, 2) * 16 + lax.rem(x + dx, 4) * 4 + lax.rem(y + dy, 4)
        for dz, dx, dy in OFFSETS
    ]

    barrier = pltpu.get_barrier_semaphore()
    for peer in peers:
        pl.semaphore_signal(barrier, inc=1, device_id=(peer, ch), device_id_type=MESH)

    loads = [
        pltpu.make_async_copy(src, dst, table_sem.at[i])
        for i, (src, dst) in enumerate(
            (
                (outer_hbm, outer3), (re_hbm, turn_re), (im_hbm, turn_im),
                (inner_hbm, inner3), (back_hbm, back3),
            )
        )
    ]
    for load in loads:
        load.start()

    def prepare(chunk):
        lanes = pl.ds(chunk * SIDE, SIDE)
        signals = (
            k_ref[:, lanes] * v_ref[:, lanes],
            f_ref[:, lanes],
            g_ref[:, lanes] * q_ref[:, lanes],
        )
        for sig, values in enumerate(signals):
            outgoing[chunk, :, sig] = values.T.reshape(BLOCKS, CHUNK, ROW)
        arrived[chunk, ctx] = outgoing[chunk, ctx]

    def go(chunk, i):
        return pltpu.make_async_remote_copy(
            outgoing.at[chunk, peers[i]], arrived.at[chunk, ctx],
            go_send.at[chunk, i], go_recv.at[chunk, i],
            device_id=(peers[i], ch), device_id_type=MESH,
        )

    def come(chunk, i):
        return pltpu.make_async_remote_copy(
            results.at[chunk, peers[i]], returned.at[chunk, ctx],
            back_send.at[chunk, i], back_recv.at[chunk, i],
            device_id=(peers[i], ch), device_id_type=MESH,
        )

    def own(chunk):
        return pltpu.make_async_copy(
            results.at[chunk, ctx], returned.at[chunk, ctx], own_sem.at[chunk]
        )

    for chunk in range(CHUNKS):
        prepare(chunk)
        if chunk == 0:
            pl.semaphore_wait(barrier, PEERS)
        for i in range(PEERS):
            go(chunk, i).start()
    for load in loads:
        load.wait()
    for chunk in range(CHUNKS):
        for i in range(PEERS):
            go(chunk, i).wait_recv()
        transform(
            arrived.at[chunk], results.at[chunk], outer3, turn_re, turn_im, inner3, back3, wide
        )
        for i in range(PEERS):
            come(chunk, i).start()
        own(chunk).start()
    for chunk in range(CHUNKS):
        for i in range(PEERS):
            go(chunk, i).wait_send()
        own(chunk).wait()
        for i in range(PEERS):
            come(chunk, i).wait()


def exchange(query, key, value, taps, cotangent, *consts):
    vmem = pl.BlockSpec(memory_space=pltpu.VMEM)
    hbm = pl.BlockSpec(memory_space=pl.ANY)
    shape = (CHUNKS, BLOCKS, 3, CHUNK, ROW)
    return pl.pallas_call(
        exchange_kernel,
        out_shape=jax.ShapeDtypeStruct(shape, F32),
        in_specs=[vmem] * 5 + [hbm] * 5,
        out_specs=hbm,
        scratch_shapes=[
            pltpu.VMEM(shape, F32),
            pltpu.VMEM(shape, F32),
            pltpu.VMEM(shape, F32),
            pltpu.VMEM((3 * SIDE, 6 * ROW), BF16),
            *[pltpu.VMEM(c.shape, c.dtype) for c in consts],
            pltpu.SemaphoreType.DMA((5,)),
            pltpu.SemaphoreType.DMA((CHUNKS, PEERS)),
            pltpu.SemaphoreType.DMA((CHUNKS, PEERS)),
            pltpu.SemaphoreType.DMA((CHUNKS, PEERS)),
            pltpu.SemaphoreType.DMA((CHUNKS, PEERS)),
            pltpu.SemaphoreType.DMA((CHUNKS,)),
        ],
        compiler_params=pltpu.CompilerParams(
            collective_id=0, has_side_effects=True, vmem_limit_bytes=48 * 2**20
        ),
        name="exchange",
    )(query, key, value, taps, cotangent, *consts)


def gate_kernel(r_ref, q_ref, k_ref, v_ref, g_ref, out, d_query, d_key, d_value, d_taps):
    def turned(sig):
        return r_ref[0, :, sig].reshape(SIDE, -1).T

    convolved = turned(0)
    out[...] = q_ref[...] * convolved
    d_query[...] = g_ref[...] * convolved
    d_mixed = turned(1)
    d_key[...] = d_mixed * v_ref[...]
    d_value[...] = d_mixed * k_ref[...]
    d_taps[...] = turned(2)


def gate(returned, query, key, value, cotangent):
    part = 128
    block = pl.BlockSpec((part, SIDE), lambda c, p: (p, c))
    return pl.pallas_call(
        gate_kernel,
        grid=(CHUNKS, ROW // part),
        out_shape=[jax.ShapeDtypeStruct(query.shape, F32)] * 5,
        in_specs=[pl.BlockSpec((1, BLOCKS, 3, CHUNK, part), lambda c, p: (c, 0, 0, 0, p))]
        + [block] * 4,
        out_specs=[block] * 5,
        name="gate",
    )(returned, query, key, value, cotangent)


def shards(query, key, value, taps, cotangent):
    consts = [jnp.asarray(c) for c in tables()]
    returned = exchange(query, key, value, taps, cotangent, *consts)
    return tuple(gate(returned, query, key, value, cotangent))


def solution(mesh):
    placed = P("ctx", "ch")
    return jax.shard_map(
        shards,
        mesh=mesh,
        in_specs=(placed,) * 5,
        out_specs=(placed,) * 5,
        check_vma=False,
    )
```

```python
import functools
import math

import jax
import jax.numpy as jnp
import ml_dtypes
import numpy as np
from jax import lax
from jax.experimental import pallas as pl
from jax.experimental.pallas import tpu as pltpu
from jax.sharding import PartitionSpec as P

MESH = pl.DeviceIdType.MESH
BF16 = jnp.bfloat16
F32 = jnp.float32

BLOCKS = 32
PLANES = 16
ROW = 256
CHUNK = 8
CHUNKS = 4
LANES = PLANES * CHUNK
FIRST = 0
SECOND = tuple(c for c in range(CHUNKS) if c != FIRST)
SIDE = BLOCKS * CHUNK
PADDED = 2 * BLOCKS * ROW

OFFSETS = (
    (0, 1), (3, 0), (0, 3), (1, 0), (1, 1), (3, 3), (1, 3), (3, 1),
    (0, 2), (2, 0), (2, 1), (1, 2), (2, 3), (3, 2), (2, 2), (0, 0),
)
NEAR = len(OFFSETS) - 1


def split_np(values):
    high = values.astype(ml_dtypes.bfloat16)
    low = (values - high.astype(np.float64)).astype(ml_dtypes.bfloat16)
    return high, low


@functools.lru_cache(maxsize=None)
def tables():
    two_pi = 2.0 * math.pi
    half = np.arange(BLOCKS) + 0.5
    block = np.arange(BLOCKS)
    row = np.arange(ROW)
    eye = np.eye(CHUNK)
    psi = two_pi * np.outer(half, block) / (2 * BLOCKS)
    outer = np.concatenate([np.kron(np.cos(psi), eye), np.kron(-np.sin(psi), eye)], axis=0)
    high, low = split_np(outer)
    outer3 = np.concatenate([high, low, high], axis=1)
    theta = two_pi * np.outer(half, row) / PADDED
    turn_re = np.repeat(np.cos(theta), CHUNK, axis=0).astype(np.float32)
    turn_im = np.repeat(-np.sin(theta), CHUNK, axis=0).astype(np.float32)
    phi = two_pi * (np.outer(row, row) % ROW) / ROW
    inner = np.block([[np.cos(phi), -np.sin(phi)], [np.sin(phi), np.cos(phi)]])
    high, low = split_np(inner)
    inner3 = np.concatenate([high, high, low], axis=0)
    back = np.concatenate([np.kron(np.cos(psi.T), eye), np.kron(np.sin(psi.T), eye)], axis=1)
    high, low = split_np(back * (2.0 / PADDED))
    back3 = np.concatenate([high, low, high], axis=1)
    return outer3, turn_re, turn_im, inner3, back3


def halves(values):
    high = values.astype(BF16)
    return high, (values - high.astype(F32)).astype(BF16)


def transform(arrived, results, outer3, turn_re, turn_im, inner3, back3, wide):
    t_re = turn_re[...]
    t_im = turn_im[...]
    for sig in range(3):
        high, low = halves(arrived[:, sig].reshape(SIDE, ROW))
        mixed = jnp.dot(
            outer3[...], jnp.concatenate([high, high, low], axis=0), preferred_element_type=F32
        )
        z_re, z_im = mixed[:SIDE], mixed[SIDE:]
        rows = pl.ds(sig * SIDE, SIDE)
        high, low = halves(z_re * t_re - z_im * t_im)
        wide[rows, 0 * ROW : 1 * ROW] = high
        wide[rows, 2 * ROW : 3 * ROW] = low
        wide[rows, 4 * ROW : 5 * ROW] = high
        high, low = halves(z_re * t_im + z_im * t_re)
        wide[rows, 1 * ROW : 2 * ROW] = high
        wide[rows, 3 * ROW : 4 * ROW] = low
        wide[rows, 5 * ROW : 6 * ROW] = high
    spec = jnp.dot(wide[...], inner3[...], preferred_element_type=F32)
    m_re, m_im = spec[:SIDE, :ROW], spec[:SIDE, ROW:]
    h_re, h_im = spec[SIDE : 2 * SIDE, :ROW], spec[SIDE : 2 * SIDE, ROW:]
    u_re, u_im = spec[2 * SIDE :, :ROW], spec[2 * SIDE :, ROW:]
    products = (
        (m_re * h_re - m_im * h_im, -(m_re * h_im + m_im * h_re)),
        (h_re * u_re + h_im * u_im, h_im * u_re - h_re * u_im),
        (m_re * u_re + m_im * u_im, m_im * u_re - m_re * u_im),
    )
    for sig, (p_re, p_im) in enumerate(products):
        rows = pl.ds(sig * SIDE, SIDE)
        high, low = halves(p_re)
        wide[rows, 0 * ROW : 1 * ROW] = high
        wide[rows, 2 * ROW : 3 * ROW] = low
        wide[rows, 4 * ROW : 5 * ROW] = high
        high, low = halves(p_im)
        wide[rows, 1 * ROW : 2 * ROW] = high
        wide[rows, 3 * ROW : 4 * ROW] = low
        wide[rows, 5 * ROW : 6 * ROW] = high
    inv = jnp.dot(wide[...], inner3[...], preferred_element_type=F32)
    for sig in range(3):
        v_re = inv[sig * SIDE : (sig + 1) * SIDE, :ROW]
        v_im = inv[sig * SIDE : (sig + 1) * SIDE, ROW:]
        re_high, re_low = halves(v_re * t_re - v_im * t_im)
        im_high, im_low = halves(v_re * t_im + v_im * t_re)
        stacked = jnp.concatenate([re_high, im_high, re_high, im_high, re_low, im_low], axis=0)
        out = jnp.dot(back3[...], stacked, preferred_element_type=F32)
        results[:, sig] = out.reshape(BLOCKS, CHUNK, ROW)


def exchange_kernel(
    q_hbm, k_hbm, v_hbm, f_hbm, g_hbm, outer_hbm, re_hbm, im_hbm, inner_hbm, back_hbm,
    returned, extra,
    q_ref, k_ref, v_ref, f_ref, g_ref, outgoing, arrived, results,
    wide, outer3, turn_re, turn_im, inner3, back3,
    input_sem, table_sem, near_out, near_in, far_out, far_in,
    near_back, near_home, far_back, far_home, own_sem,
):
    ctx = lax.axis_index("ctx")
    ch = lax.axis_index("ch")
    half = ctx // PLANES
    place = lax.rem(ctx, PLANES)
    x = place // 4
    y = lax.rem(place, 4)
    places = [lax.rem(x + dx, 4) * 4 + lax.rem(y + dy, 4) for dx, dy in OFFSETS]
    here = half * PLANES
    there = PLANES - here

    pairs = (
        (k_hbm, k_ref), (v_hbm, v_ref), (f_hbm, f_ref), (g_hbm, g_ref), (q_hbm, q_ref)
    )
    inputs = [
        [
            pltpu.make_async_copy(
                src.at[:, pl.ds(chunk * LANES, LANES)], dst.at[chunk], input_sem.at[chunk, i]
            )
            for i, (src, dst) in enumerate(pairs)
        ]
        for chunk in range(CHUNKS)
    ]
    for load in inputs[0] + inputs[1]:
        load.start()

    barrier = pltpu.get_barrier_semaphore()
    for i in range(NEAR + 1):
        if i < NEAR:
            pl.semaphore_signal(
                barrier, inc=1, device_id=(here + places[i], ch), device_id_type=MESH
            )
        pl.semaphore_signal(
            barrier, inc=1, device_id=(there + places[i], ch), device_id_type=MESH
        )

    loads = [
        pltpu.make_async_copy(src, dst, table_sem.at[i])
        for i, (src, dst) in enumerate(
            (
                (outer_hbm, outer3), (re_hbm, turn_re), (im_hbm, turn_im),
                (inner_hbm, inner3), (back_hbm, back3),
            )
        )
    ]
    for load in inputs[2] + inputs[3] + loads:
        load.start()

    def near(chunk, i):
        return pltpu.make_async_remote_copy(
            outgoing.at[chunk, places[i]], arrived.at[chunk, ctx],
            near_out.at[chunk, i], near_in.at[chunk, i],
            device_id=(here + places[i], ch), device_id_type=MESH,
        )

    def far(chunk, i):
        count = 3 if chunk == FIRST else 2
        return pltpu.make_async_remote_copy(
            outgoing.at[chunk, places[i], pl.ds(0, count)],
            arrived.at[chunk, ctx, pl.ds(0, count)],
            far_out.at[chunk, i], far_in.at[chunk, i],
            device_id=(there + places[i], ch), device_id_type=MESH,
        )

    def near_return(chunk, i):
        return pltpu.make_async_remote_copy(
            results.at[chunk, here + places[i]], returned.at[chunk, place],
            near_back.at[chunk, i], near_home.at[chunk, i],
            device_id=(here + places[i], ch), device_id_type=MESH,
        )

    def far_return(chunk, i):
        if chunk == FIRST:
            src, dst = results.at[chunk, there + places[i]], returned.at[chunk, place]
        else:
            src = results.at[chunk, there + places[i], pl.ds(1, 2)]
            dst = extra.at[chunk, place]
        return pltpu.make_async_remote_copy(
            src, dst, far_back.at[chunk, i], far_home.at[chunk, i],
            device_id=(there + places[i], ch), device_id_type=MESH,
        )

    def own(chunk):
        return pltpu.make_async_copy(
            results.at[chunk, ctx], returned.at[chunk, place], own_sem.at[chunk]
        )

    def prepare(chunk):
        for load in inputs[chunk]:
            load.wait()
        signals = (k_ref[chunk] * v_ref[chunk], f_ref[chunk], g_ref[chunk] * q_ref[chunk])
        for sig, values in enumerate(signals):
            outgoing[chunk, :, sig] = values.T.reshape(PLANES, CHUNK, ROW)
        if chunk == FIRST:

            @pl.when(half == 0)
            def _():
                arrived[chunk, ctx] = outgoing[chunk, place]
        else:
            arrived[chunk, ctx] = outgoing[chunk, place]

    def start(copies):
        for copy in copies:
            copy.start()

    def mingle(first, second):
        order = []
        for i in range(NEAR + 1):
            order.append(first(i))
            if i < NEAR:
                order.append(second(i))
        return order

    def relay(done, follow):
        for i in range(NEAR + 1):
            done(i).wait_send()
            follow(i).start()

    def of(make, chunk):
        return functools.partial(make, chunk)

    def every(make, chunk):
        return [make(chunk, i) for i in range(NEAR)]

    def first_half(body):
        pl.when(half == 0)(body)

    def second_half(body):
        pl.when(half == 1)(body)

    @first_half
    def _():
        prepare(1)
        pl.semaphore_wait(barrier, 2 * NEAR + 1)
        prepare(0)
        start(mingle(of(far, 1), of(near, 0)))
        prepare(2)
        prepare(3)
        start(every(near, 1))
        for chunk in SECOND:
            arrived[chunk, PLANES:] = jnp.zeros((PLANES, 3, CHUNK, ROW), F32)

    @second_half
    def _():
        prepare(0)
        pl.semaphore_wait(barrier, 2 * NEAR + 1)
        prepare(1)
        start(mingle(of(far, 0), of(near, 1)))
        prepare(2)
        start(every(near, 2))
        prepare(3)
        start(every(near, 3))
        for chunk in SECOND:
            arrived[chunk, :PLANES, 2] = jnp.zeros((PLANES, CHUNK, ROW), F32)

    for load in loads:
        load.wait()

    def work(chunk):
        for i in range(NEAR):
            near(chunk, i).wait_recv()
        transform(
            arrived.at[chunk], results.at[chunk], outer3, turn_re, turn_im, inner3, back3, wide
        )
        start(every(near_return, chunk))
        own(chunk).start()

    def arrive(make, chunk):
        for i in range(NEAR + 1):
            make(chunk, i).wait_recv()

    @first_half
    def _():
        relay(of(far, 1), of(far, 2))
        start(every(near, 2))
        arrive(far, 0)
        work(0)
        relay(of(far, 2), of(far, 3))
        start(every(near, 3))

    second_half(lambda: arrive(far, 1))
    work(1)
    second_half(lambda: relay(of(far, 0), of(far_return, 1)))

    second_half(lambda: arrive(far, 2))
    work(2)
    first_half(lambda: relay(of(far, 3), of(far_return, 0)))
    second_half(lambda: relay(of(far_return, 1), of(far_return, 2)))

    second_half(lambda: arrive(far, 3))
    work(3)
    second_half(lambda: relay(of(far_return, 2), of(far_return, 3)))

    def finish(chunk):
        for i in range(NEAR):
            near(chunk, i).wait_send()
            near_return(chunk, i).wait()
        own(chunk).wait()

    for chunk in SECOND:
        finish(chunk)

    @first_half
    def _():
        finish(0)
        for chunk in SECOND:
            arrive(far_return, chunk)
        for i in range(NEAR + 1):
            far_return(0, i).wait_send()

    @second_half
    def _():
        arrive(far_return, 0)
        for i in range(NEAR + 1):
            far_return(3, i).wait_send()


def exchange(query, key, value, taps, cotangent, *consts):
    hbm = pl.BlockSpec(memory_space=pl.ANY)
    signals = pltpu.VMEM((CHUNKS, BLOCKS, 3, CHUNK, ROW), F32)
    near_sem = pltpu.SemaphoreType.DMA((CHUNKS, NEAR))
    far_sem = pltpu.SemaphoreType.DMA((CHUNKS, NEAR + 1))
    return pl.pallas_call(
        exchange_kernel,
        out_shape=[
            jax.ShapeDtypeStruct((CHUNKS, PLANES, 3, CHUNK, ROW), F32),
            jax.ShapeDtypeStruct((CHUNKS, PLANES, 2, CHUNK, ROW), F32),
        ],
        in_specs=[hbm] * 10,
        out_specs=[hbm] * 2,
        scratch_shapes=[
            *[pltpu.VMEM((CHUNKS, ROW, LANES), F32)] * 5,
            pltpu.VMEM((CHUNKS, PLANES, 3, CHUNK, ROW), F32),
            signals,
            signals,
            pltpu.VMEM((3 * SIDE, 6 * ROW), BF16),
            *[pltpu.VMEM(c.shape, c.dtype) for c in consts],
            pltpu.SemaphoreType.DMA((CHUNKS, 5)),
            pltpu.SemaphoreType.DMA((5,)),
            near_sem, near_sem, far_sem, far_sem, near_sem, near_sem, far_sem, far_sem,
            pltpu.SemaphoreType.DMA((CHUNKS,)),
        ],
        compiler_params=pltpu.CompilerParams(
            collective_id=0, has_side_effects=True, vmem_limit_bytes=60 * 2**20
        ),
        name="exchange",
    )(query, key, value, taps, cotangent, *consts)


def gate_kernel(r_ref, e_ref, q_ref, k_ref, v_ref, g_ref, out, d_query, d_key, d_value, d_taps):
    chunk = pl.program_id(0)
    shared = jnp.logical_and(lax.axis_index("ctx") < PLANES, chunk != FIRST)

    def turned(ref, sig):
        return ref[0, :, sig].reshape(LANES, -1).T

    def summed(sig):
        mine = turned(r_ref, sig)
        return jnp.where(shared, mine + turned(e_ref, sig - 1), mine)

    convolved = turned(r_ref, 0)
    out[...] = q_ref[...] * convolved
    d_query[...] = g_ref[...] * convolved
    d_mixed = summed(1)
    d_key[...] = d_mixed * v_ref[...]
    d_value[...] = d_mixed * k_ref[...]
    d_taps[...] = summed(2)


def gate(returned, extra, query, key, value, cotangent):
    block = pl.BlockSpec((ROW, LANES), lambda c: (0, c))
    return pl.pallas_call(
        gate_kernel,
        grid=(CHUNKS,),
        out_shape=[jax.ShapeDtypeStruct(query.shape, F32)] * 5,
        in_specs=[
            pl.BlockSpec((1, PLANES, 3, CHUNK, ROW), lambda c: (c, 0, 0, 0, 0)),
            pl.BlockSpec(
                (1, PLANES, 2, CHUNK, ROW),
                lambda c: (jnp.where(c == FIRST, FIRST + 1, c), 0, 0, 0, 0),
            ),
        ]
        + [block] * 4,
        out_specs=[block] * 5,
        name="gate",
    )(returned, extra, query, key, value, cotangent)


def shards(query, key, value, taps, cotangent):
    consts = [jnp.asarray(c) for c in tables()]
    returned, extra = exchange(query, key, value, taps, cotangent, *consts)
    return tuple(gate(returned, extra, query, key, value, cotangent))


def solution(mesh):
    placed = P("ctx", "ch")
    return jax.shard_map(
        shards,
        mesh=mesh,
        in_specs=(placed,) * 5,
        out_specs=(placed,) * 5,
        check_vma=False,
    )
```

```python
import functools
import math

import jax
import jax.numpy as jnp
import ml_dtypes
import numpy as np
from jax import lax
from jax.experimental import pallas as pl
from jax.experimental.pallas import tpu as pltpu
from jax.sharding import PartitionSpec as P

MESH = pl.DeviceIdType.MESH
BF16 = jnp.bfloat16
F32 = jnp.float32

BLOCKS = 32
PLANES = 16
ROW = 256
CHUNK = 8
CHUNKS = 4
LANES = PLANES * CHUNK
FIRST = 0
SECOND = tuple(c for c in range(CHUNKS) if c != FIRST)
SIDE = BLOCKS * CHUNK
PADDED = 2 * BLOCKS * ROW

OFFSETS = (
    (0, 1), (3, 0), (0, 3), (1, 0), (1, 1), (3, 3), (1, 3), (3, 1),
    (0, 2), (2, 0), (2, 1), (1, 2), (2, 3), (3, 2), (2, 2), (0, 0),
)
NEAR = len(OFFSETS) - 1
COLUMN = 8
PIECES = (tuple(range(8)), tuple(range(8, NEAR + 1)))


def split_np(values):
    high = values.astype(ml_dtypes.bfloat16)
    low = (values - high.astype(np.float64)).astype(ml_dtypes.bfloat16)
    return high, low


@functools.lru_cache(maxsize=None)
def tables():
    two_pi = 2.0 * math.pi
    half = np.arange(BLOCKS) + 0.5
    block = np.arange(BLOCKS)
    row = np.arange(ROW)
    eye = np.eye(CHUNK)
    psi = two_pi * np.outer(half, block) / (2 * BLOCKS)
    outer = np.concatenate([np.kron(np.cos(psi), eye), np.kron(-np.sin(psi), eye)], axis=0)
    high, low = split_np(outer)
    outer3 = np.concatenate([high, low, high], axis=1)
    theta = two_pi * np.outer(half, row) / PADDED
    turn_re = np.repeat(np.cos(theta), CHUNK, axis=0).astype(np.float32)
    turn_im = np.repeat(-np.sin(theta), CHUNK, axis=0).astype(np.float32)
    phi = two_pi * (np.outer(row, row) % ROW) / ROW
    inner = np.block([[np.cos(phi), -np.sin(phi)], [np.sin(phi), np.cos(phi)]])
    high, low = split_np(inner)
    inner3 = np.concatenate([high, high, low], axis=0)
    back = np.concatenate([np.kron(np.cos(psi.T), eye), np.kron(np.sin(psi.T), eye)], axis=1)
    high, low = split_np(back * (2.0 / PADDED))
    back3 = np.concatenate([high, low, high], axis=1)
    return outer3, turn_re, turn_im, inner3, back3


def halves(values):
    high = values.astype(BF16)
    return high, (values - high.astype(F32)).astype(BF16)


def transform(arrived, results, outer3, turn_re, turn_im, inner3, back3, wide):
    t_re = turn_re[...]
    t_im = turn_im[...]
    for sig in range(3):
        high, low = halves(arrived[:, sig].reshape(SIDE, ROW))
        mixed = jnp.dot(
            outer3[...], jnp.concatenate([high, high, low], axis=0), preferred_element_type=F32
        )
        z_re, z_im = mixed[:SIDE], mixed[SIDE:]
        rows = pl.ds(sig * SIDE, SIDE)
        high, low = halves(z_re * t_re - z_im * t_im)
        wide[rows, 0 * ROW : 1 * ROW] = high
        wide[rows, 2 * ROW : 3 * ROW] = low
        wide[rows, 4 * ROW : 5 * ROW] = high
        high, low = halves(z_re * t_im + z_im * t_re)
        wide[rows, 1 * ROW : 2 * ROW] = high
        wide[rows, 3 * ROW : 4 * ROW] = low
        wide[rows, 5 * ROW : 6 * ROW] = high
    spec = jnp.dot(wide[...], inner3[...], preferred_element_type=F32)
    m_re, m_im = spec[:SIDE, :ROW], spec[:SIDE, ROW:]
    h_re, h_im = spec[SIDE : 2 * SIDE, :ROW], spec[SIDE : 2 * SIDE, ROW:]
    u_re, u_im = spec[2 * SIDE :, :ROW], spec[2 * SIDE :, ROW:]
    products = (
        (m_re * h_re - m_im * h_im, -(m_re * h_im + m_im * h_re)),
        (h_re * u_re + h_im * u_im, h_im * u_re - h_re * u_im),
        (m_re * u_re + m_im * u_im, m_im * u_re - m_re * u_im),
    )
    for sig, (p_re, p_im) in enumerate(products):
        rows = pl.ds(sig * SIDE, SIDE)
        high, low = halves(p_re)
        wide[rows, 0 * ROW : 1 * ROW] = high
        wide[rows, 2 * ROW : 3 * ROW] = low
        wide[rows, 4 * ROW : 5 * ROW] = high
        high, low = halves(p_im)
        wide[rows, 1 * ROW : 2 * ROW] = high
        wide[rows, 3 * ROW : 4 * ROW] = low
        wide[rows, 5 * ROW : 6 * ROW] = high
    inv = jnp.dot(wide[...], inner3[...], preferred_element_type=F32)
    for sig in range(3):
        v_re = inv[sig * SIDE : (sig + 1) * SIDE, :ROW]
        v_im = inv[sig * SIDE : (sig + 1) * SIDE, ROW:]
        re_high, re_low = halves(v_re * t_re - v_im * t_im)
        im_high, im_low = halves(v_re * t_im + v_im * t_re)
        stacked = jnp.concatenate([re_high, im_high, re_high, im_high, re_low, im_low], axis=0)
        out = jnp.dot(back3[...], stacked, preferred_element_type=F32)
        results[:, sig] = out.reshape(BLOCKS, CHUNK, ROW)


def exchange_kernel(
    q_hbm, k_hbm, v_hbm, f_hbm, g_hbm, outer_hbm, re_hbm, im_hbm, inner_hbm, back_hbm,
    returned, extra,
    q_ref, k_ref, v_ref, f_ref, g_ref, outgoing, arrived, results,
    wide, outer3, turn_re, turn_im, inner3, back3,
    input_sem, table_sem, near_out, near_in, far_out, far_in,
    near_back, near_home, far_back, far_home, own_sem, credit,
):
    ctx = lax.axis_index("ctx")
    ch = lax.axis_index("ch")
    half = ctx // PLANES
    place = lax.rem(ctx, PLANES)
    x = place // 4
    y = lax.rem(place, 4)
    places = [lax.rem(x + dx, 4) * 4 + lax.rem(y + dy, 4) for dx, dy in OFFSETS]
    here = half * PLANES
    there = PLANES - here

    pairs = (
        (k_hbm, k_ref), (v_hbm, v_ref), (f_hbm, f_ref), (g_hbm, g_ref), (q_hbm, q_ref)
    )
    inputs = [
        [
            pltpu.make_async_copy(
                src.at[:, pl.ds(chunk * LANES, LANES)], dst.at[chunk], input_sem.at[chunk, i]
            )
            for i, (src, dst) in enumerate(pairs)
        ]
        for chunk in range(CHUNKS)
    ]
    for load in inputs[0] + inputs[1]:
        load.start()

    barrier = pltpu.get_barrier_semaphore()
    for i in range(NEAR + 1):
        if i < NEAR:
            pl.semaphore_signal(
                barrier, inc=1, device_id=(here + places[i], ch), device_id_type=MESH
            )
        pl.semaphore_signal(
            barrier, inc=1, device_id=(there + places[i], ch), device_id_type=MESH
        )
    for k in range(1, COLUMN):
        pl.semaphore_signal(
            barrier, inc=1, device_id=(there + place, lax.rem(ch + k, COLUMN)),
            device_id_type=MESH,
        )

    loads = [
        pltpu.make_async_copy(src, dst, table_sem.at[i])
        for i, (src, dst) in enumerate(
            (
                (outer_hbm, outer3), (re_hbm, turn_re), (im_hbm, turn_im),
                (inner_hbm, inner3), (back_hbm, back3),
            )
        )
    ]
    for load in inputs[2] + inputs[3] + loads:
        load.start()

    def near(chunk, i):
        return pltpu.make_async_remote_copy(
            outgoing.at[chunk, places[i]], arrived.at[chunk, ctx],
            near_out.at[chunk, i], near_in.at[chunk, i],
            device_id=(here + places[i], ch), device_id_type=MESH,
        )

    def far(chunk, i):
        count = 3 if chunk == FIRST else 2
        return pltpu.make_async_remote_copy(
            outgoing.at[chunk, places[i], pl.ds(0, count)],
            arrived.at[chunk, ctx, pl.ds(0, count)],
            far_out.at[chunk, i], far_in.at[chunk, i],
            device_id=(there + places[i], ch), device_id_type=MESH,
        )

    def near_return(chunk, i):
        return pltpu.make_async_remote_copy(
            results.at[chunk, here + places[i]], returned.at[chunk, place],
            near_back.at[chunk, i], near_home.at[chunk, i],
            device_id=(here + places[i], ch), device_id_type=MESH,
        )

    def far_return(chunk, i):
        if chunk == FIRST:
            src, dst = results.at[chunk, there + places[i]], returned.at[chunk, place]
        else:
            src = results.at[chunk, there + places[i], pl.ds(1, 2)]
            dst = extra.at[chunk, place]
        return pltpu.make_async_remote_copy(
            src, dst, far_back.at[chunk, i], far_home.at[chunk, i],
            device_id=(there + places[i], ch), device_id_type=MESH,
        )

    def own(chunk):
        return pltpu.make_async_copy(
            results.at[chunk, ctx], returned.at[chunk, place], own_sem.at[chunk]
        )

    def prepare(chunk):
        for load in inputs[chunk]:
            load.wait()
        signals = (k_ref[chunk] * v_ref[chunk], f_ref[chunk], g_ref[chunk] * q_ref[chunk])
        for sig, values in enumerate(signals):
            outgoing[chunk, :, sig] = values.T.reshape(PLANES, CHUNK, ROW)
        if chunk == FIRST:

            @pl.when(half == 0)
            def _():
                arrived[chunk, ctx] = outgoing[chunk, place]
        else:
            arrived[chunk, ctx] = outgoing[chunk, place]

    def start(copies):
        for copy in copies:
            copy.start()

    def every(make, chunk):
        return [make(chunk, i) for i in range(NEAR)]

    def part(make, chunk, piece):
        return [make(chunk, i) for i in PIECES[piece]]

    def grant(step):
        for k in range(COLUMN):
            pl.semaphore_signal(
                credit.at[step], inc=1, device_id=(place, lax.rem(ch + k, COLUMN)),
                device_id_type=MESH,
            )

    def granted(step, copies):
        pl.semaphore_wait(credit.at[step], COLUMN)
        start(copies)

    def first_half(body):
        pl.when(half == 0)(body)

    def second_half(body):
        pl.when(half == 1)(body)

    def all_far(make, chunk):
        return [make(chunk, i) for i in range(NEAR + 1)]

    @first_half
    def _():
        prepare(1)
        pl.semaphore_wait(barrier, 2 * NEAR + COLUMN)
        start(all_far(far, 1))
        prepare(0)
        start(every(near, 0))
        prepare(2)
        prepare(3)
        start(every(near, 1))
        for chunk in SECOND:
            arrived[chunk, PLANES:] = jnp.zeros((PLANES, 3, CHUNK, ROW), F32)

    @second_half
    def _():
        prepare(0)
        pl.semaphore_wait(barrier, 2 * NEAR + COLUMN)
        start(all_far(far, 0))
        prepare(1)
        start(every(near, 1))
        prepare(2)
        start(every(near, 2))
        prepare(3)
        start(every(near, 3))
        for chunk in SECOND:
            arrived[chunk, :PLANES, 2] = jnp.zeros((PLANES, CHUNK, ROW), F32)

    for load in loads:
        load.wait()

    def work(chunk):
        for i in range(NEAR):
            near(chunk, i).wait_recv()
        transform(
            arrived.at[chunk], results.at[chunk], outer3, turn_re, turn_im, inner3, back3, wide
        )
        start(every(near_return, chunk))
        own(chunk).start()

    def arrive(make, chunk):
        for i in range(NEAR + 1):
            make(chunk, i).wait_recv()

    def relay(done, follow):
        for before, after in zip(done, follow):
            before.wait_send()
            after.start()

    @first_half
    def _():
        relay(all_far(far, 1), all_far(far, 2))
        start(every(near, 2))
        granted(0, all_far(far, 3))
        start(every(near, 3))
        arrive(far, 0)
        work(0)

    def come(chunk):
        arrive(far, chunk)
        if chunk == 1:
            grant(0)
        if chunk == 2:
            grant(1)

    second_half(lambda: come(1))
    work(1)
    second_half(lambda: start(all_far(far_return, 1)))
    first_half(lambda: granted(1, all_far(far_return, 0)))

    second_half(lambda: come(2))
    work(2)
    second_half(lambda: start(all_far(far_return, 2)))

    second_half(lambda: come(3))
    work(3)
    second_half(lambda: start(all_far(far_return, 3)))

    def finish(chunk):
        for i in range(NEAR):
            near(chunk, i).wait_send()
            near_return(chunk, i).wait()
        own(chunk).wait()

    for chunk in SECOND:
        finish(chunk)

    @first_half
    def _():
        finish(0)
        for chunk in SECOND:
            arrive(far_return, chunk)
            if chunk > 1:
                for copy in all_far(far, chunk):
                    copy.wait_send()
        for copy in all_far(far_return, 0):
            copy.wait_send()

    @second_half
    def _():
        arrive(far_return, 0)
        for copy in all_far(far, 0):
            copy.wait_send()
        for chunk in SECOND:
            for copy in all_far(far_return, chunk):
                copy.wait_send()


def exchange(query, key, value, taps, cotangent, *consts):
    hbm = pl.BlockSpec(memory_space=pl.ANY)
    signals = pltpu.VMEM((CHUNKS, BLOCKS, 3, CHUNK, ROW), F32)
    near_sem = pltpu.SemaphoreType.DMA((CHUNKS, NEAR))
    far_sem = pltpu.SemaphoreType.DMA((CHUNKS, NEAR + 1))
    return pl.pallas_call(
        exchange_kernel,
        out_shape=[
            jax.ShapeDtypeStruct((CHUNKS, PLANES, 3, CHUNK, ROW), F32),
            jax.ShapeDtypeStruct((CHUNKS, PLANES, 2, CHUNK, ROW), F32),
        ],
        in_specs=[hbm] * 10,
        out_specs=[hbm] * 2,
        scratch_shapes=[
            *[pltpu.VMEM((CHUNKS, ROW, LANES), F32)] * 5,
            pltpu.VMEM((CHUNKS, PLANES, 3, CHUNK, ROW), F32),
            signals,
            signals,
            pltpu.VMEM((3 * SIDE, 6 * ROW), BF16),
            *[pltpu.VMEM(c.shape, c.dtype) for c in consts],
            pltpu.SemaphoreType.DMA((CHUNKS, 5)),
            pltpu.SemaphoreType.DMA((5,)),
            near_sem, near_sem, far_sem, far_sem, near_sem, near_sem, far_sem, far_sem,
            pltpu.SemaphoreType.DMA((CHUNKS,)),
            pltpu.SemaphoreType.REGULAR((2,)),
        ],
        compiler_params=pltpu.CompilerParams(
            collective_id=0, has_side_effects=True, vmem_limit_bytes=60 * 2**20
        ),
        name="exchange",
    )(query, key, value, taps, cotangent, *consts)


def gate_kernel(r_hbm, e_hbm, q_hbm, k_hbm, v_hbm, g_hbm, *rest):
    outs_hbm = rest[:5]
    r_ref, e_ref, q_ref, k_ref, v_ref, g_ref = rest[5:11]
    outs = rest[11:16]
    load_sem, store_sem = rest[16:]
    shared = lax.axis_index("ctx") < PLANES

    def lanes(ref, chunk):
        return ref.at[:, pl.ds(chunk * LANES, LANES)]

    def loads(chunk):
        pairs = [(r_hbm.at[chunk], r_ref.at[chunk])]
        if chunk != FIRST:
            pairs.append((e_hbm.at[chunk], e_ref.at[chunk]))
        for src, dst in ((q_hbm, q_ref), (g_hbm, g_ref), (v_hbm, v_ref), (k_hbm, k_ref)):
            pairs.append((lanes(src, chunk), dst.at[chunk]))
        return [
            pltpu.make_async_copy(src, dst, load_sem.at[chunk, i])
            for i, (src, dst) in enumerate(pairs)
        ]

    def stores(chunk):
        return [
            pltpu.make_async_copy(src.at[chunk], lanes(dst, chunk), store_sem.at[chunk, i])
            for i, (src, dst) in enumerate(zip(outs, outs_hbm))
        ]

    for chunk in range(CHUNKS):
        for load in loads(chunk):
            load.start()
    out, d_query, d_key, d_value, d_taps = outs
    for chunk in range(CHUNKS):
        for load in loads(chunk):
            load.wait()

        def summed(sig):
            mine = r_ref[chunk, :, sig]
            if chunk != FIRST:
                mine = jnp.where(shared, mine + e_ref[chunk, :, sig - 1], mine)
            return mine.reshape(LANES, ROW).T

        convolved = r_ref[chunk, :, 0].reshape(LANES, ROW).T
        out[chunk] = q_ref[chunk] * convolved
        d_query[chunk] = g_ref[chunk] * convolved
        d_mixed = summed(1)
        d_key[chunk] = d_mixed * v_ref[chunk]
        d_value[chunk] = d_mixed * k_ref[chunk]
        d_taps[chunk] = summed(2)
        for store in stores(chunk):
            store.start()
    for chunk in range(CHUNKS):
        for store in stores(chunk):
            store.wait()


def gate(returned, extra, query, key, value, cotangent):
    hbm = pl.BlockSpec(memory_space=pl.ANY)
    return pl.pallas_call(
        gate_kernel,
        out_shape=[jax.ShapeDtypeStruct(query.shape, F32)] * 5,
        in_specs=[hbm] * 6,
        out_specs=[hbm] * 5,
        scratch_shapes=[
            pltpu.VMEM(returned.shape, F32),
            pltpu.VMEM(extra.shape, F32),
            *[pltpu.VMEM((CHUNKS, ROW, LANES), F32)] * 9,
            pltpu.SemaphoreType.DMA((CHUNKS, 6)),
            pltpu.SemaphoreType.DMA((CHUNKS, 5)),
        ],
        compiler_params=pltpu.CompilerParams(vmem_limit_bytes=60 * 2**20),
        name="gate",
    )(returned, extra, query, key, value, cotangent)


def shards(query, key, value, taps, cotangent):
    consts = [jnp.asarray(c) for c in tables()]
    returned, extra = exchange(query, key, value, taps, cotangent, *consts)
    return tuple(gate(returned, extra, query, key, value, cotangent))


def solution(mesh):
    placed = P("ctx", "ch")
    return jax.shard_map(
        shards,
        mesh=mesh,
        in_specs=(placed,) * 5,
        out_specs=(placed,) * 5,
        check_vma=False,
    )
```

```python
import functools
import math

import jax
import jax.numpy as jnp
import ml_dtypes
import numpy as np
from jax import lax
from jax.experimental import pallas as pl
from jax.experimental.pallas import tpu as pltpu
from jax.sharding import PartitionSpec as P

MESH = pl.DeviceIdType.MESH
BF16 = jnp.bfloat16
F32 = jnp.float32

BLOCKS = 32
PLANES = 16
ROW = 256
CHUNK = 8
CHUNKS = 4
LANES = PLANES * CHUNK
FIRST = 0
SECOND = tuple(c for c in range(CHUNKS) if c != FIRST)
SIDE = BLOCKS * CHUNK
PADDED = 2 * BLOCKS * ROW

OFFSETS = (
    (2, 2), (1, 0), (0, 1), (2, 1), (3, 0), (0, 3), (2, 3), (1, 1),
    (0, 2), (3, 3), (1, 2), (3, 1), (2, 0), (1, 3), (3, 2), (0, 0),
)
NEAR = len(OFFSETS) - 1
COLUMN = 8
PIECES = (tuple(range(8)), tuple(range(8, NEAR + 1)))


def split_np(values):
    high = values.astype(ml_dtypes.bfloat16)
    low = (values - high.astype(np.float64)).astype(ml_dtypes.bfloat16)
    return high, low


@functools.lru_cache(maxsize=None)
def tables():
    two_pi = 2.0 * math.pi
    half = np.arange(BLOCKS) + 0.5
    block = np.arange(BLOCKS)
    row = np.arange(ROW)
    eye = np.eye(CHUNK)
    psi = two_pi * np.outer(half, block) / (2 * BLOCKS)
    outer = np.concatenate([np.kron(np.cos(psi), eye), np.kron(-np.sin(psi), eye)], axis=0)
    high, low = split_np(outer)
    outer3 = np.concatenate([high, low, high], axis=1)
    theta = two_pi * np.outer(half, row) / PADDED
    turn_re = np.repeat(np.cos(theta), CHUNK, axis=0).astype(np.float32)
    turn_im = np.repeat(-np.sin(theta), CHUNK, axis=0).astype(np.float32)
    phi = two_pi * (np.outer(row, row) % ROW) / ROW
    inner = np.block([[np.cos(phi), -np.sin(phi)], [np.sin(phi), np.cos(phi)]])
    high, low = split_np(inner)
    inner3 = np.concatenate([high, high, low], axis=0)
    back = np.concatenate([np.kron(np.cos(psi.T), eye), np.kron(np.sin(psi.T), eye)], axis=1)
    high, low = split_np(back * (2.0 / PADDED))
    back3 = np.concatenate([high, low, high], axis=1)
    return outer3, turn_re, turn_im, inner3, back3


def halves(values):
    high = values.astype(BF16)
    return high, (values - high.astype(F32)).astype(BF16)


def transform(arrived, results, outer3, turn_re, turn_im, inner3, back3, wide):
    t_re = turn_re[...]
    t_im = turn_im[...]
    for sig in range(3):
        high, low = halves(arrived[:, sig].reshape(SIDE, ROW))
        mixed = jnp.dot(
            outer3[...], jnp.concatenate([high, high, low], axis=0), preferred_element_type=F32
        )
        z_re, z_im = mixed[:SIDE], mixed[SIDE:]
        rows = pl.ds(sig * SIDE, SIDE)
        high, low = halves(z_re * t_re - z_im * t_im)
        wide[rows, 0 * ROW : 1 * ROW] = high
        wide[rows, 2 * ROW : 3 * ROW] = low
        wide[rows, 4 * ROW : 5 * ROW] = high
        high, low = halves(z_re * t_im + z_im * t_re)
        wide[rows, 1 * ROW : 2 * ROW] = high
        wide[rows, 3 * ROW : 4 * ROW] = low
        wide[rows, 5 * ROW : 6 * ROW] = high
    spec = jnp.dot(wide[...], inner3[...], preferred_element_type=F32)
    m_re, m_im = spec[:SIDE, :ROW], spec[:SIDE, ROW:]
    h_re, h_im = spec[SIDE : 2 * SIDE, :ROW], spec[SIDE : 2 * SIDE, ROW:]
    u_re, u_im = spec[2 * SIDE :, :ROW], spec[2 * SIDE :, ROW:]
    products = (
        (m_re * h_re - m_im * h_im, -(m_re * h_im + m_im * h_re)),
        (h_re * u_re + h_im * u_im, h_im * u_re - h_re * u_im),
        (m_re * u_re + m_im * u_im, m_im * u_re - m_re * u_im),
    )
    for sig, (p_re, p_im) in enumerate(products):
        rows = pl.ds(sig * SIDE, SIDE)
        high, low = halves(p_re)
        wide[rows, 0 * ROW : 1 * ROW] = high
        wide[rows, 2 * ROW : 3 * ROW] = low
        wide[rows, 4 * ROW : 5 * ROW] = high
        high, low = halves(p_im)
        wide[rows, 1 * ROW : 2 * ROW] = high
        wide[rows, 3 * ROW : 4 * ROW] = low
        wide[rows, 5 * ROW : 6 * ROW] = high
    inv = jnp.dot(wide[...], inner3[...], preferred_element_type=F32)
    for sig in range(3):
        v_re = inv[sig * SIDE : (sig + 1) * SIDE, :ROW]
        v_im = inv[sig * SIDE : (sig + 1) * SIDE, ROW:]
        re_high, re_low = halves(v_re * t_re - v_im * t_im)
        im_high, im_low = halves(v_re * t_im + v_im * t_re)
        stacked = jnp.concatenate([re_high, im_high, re_high, im_high, re_low, im_low], axis=0)
        out = jnp.dot(back3[...], stacked, preferred_element_type=F32)
        results[:, sig] = out.reshape(BLOCKS, CHUNK, ROW)


def exchange_kernel(
    q_hbm, k_hbm, v_hbm, f_hbm, g_hbm, outer_hbm, re_hbm, im_hbm, inner_hbm, back_hbm,
    returned, extra,
    q_ref, k_ref, v_ref, f_ref, g_ref, outgoing, arrived, results,
    wide, outer3, turn_re, turn_im, inner3, back3,
    input_sem, table_sem, near_out, near_in, far_out, far_in,
    near_back, near_home, far_back, far_home, own_sem, credit,
):
    ctx = lax.axis_index("ctx")
    ch = lax.axis_index("ch")
    half = ctx // PLANES
    place = lax.rem(ctx, PLANES)
    x = place // 4
    y = lax.rem(place, 4)
    places = [lax.rem(x + dx, 4) * 4 + lax.rem(y + dy, 4) for dx, dy in OFFSETS]
    here = half * PLANES
    there = PLANES - here

    pairs = (
        (k_hbm, k_ref), (v_hbm, v_ref), (f_hbm, f_ref), (g_hbm, g_ref), (q_hbm, q_ref)
    )
    inputs = [
        [
            pltpu.make_async_copy(
                src.at[:, pl.ds(chunk * LANES, LANES)], dst.at[chunk], input_sem.at[chunk, i]
            )
            for i, (src, dst) in enumerate(pairs)
        ]
        for chunk in range(CHUNKS)
    ]
    def start(copies):
        for copy in copies:
            copy.start()

    def first_half(body):
        pl.when(half == 0)(body)

    def second_half(body):
        pl.when(half == 1)(body)

    first_half(lambda: start(inputs[1]))
    second_half(lambda: start(inputs[0]))

    barrier = pltpu.get_barrier_semaphore()
    for i in range(NEAR + 1):
        if i < NEAR:
            pl.semaphore_signal(
                barrier, inc=1, device_id=(here + places[i], ch), device_id_type=MESH
            )
        pl.semaphore_signal(
            barrier, inc=1, device_id=(there + places[i], ch), device_id_type=MESH
        )
    for k in range(1, COLUMN):
        pl.semaphore_signal(
            barrier, inc=1, device_id=(there + place, lax.rem(ch + k, COLUMN)),
            device_id_type=MESH,
        )

    loads = [
        pltpu.make_async_copy(src, dst, table_sem.at[i])
        for i, (src, dst) in enumerate(
            (
                (outer_hbm, outer3), (re_hbm, turn_re), (im_hbm, turn_im),
                (inner_hbm, inner3), (back_hbm, back3),
            )
        )
    ]
    first_half(lambda: start(inputs[0]))
    second_half(lambda: start(inputs[1]))

    def near(chunk, i):
        return pltpu.make_async_remote_copy(
            outgoing.at[chunk, places[i]], arrived.at[chunk, ctx],
            near_out.at[chunk, i], near_in.at[chunk, i],
            device_id=(here + places[i], ch), device_id_type=MESH,
        )

    def far(chunk, i):
        count = 3 if chunk == FIRST else 2
        return pltpu.make_async_remote_copy(
            outgoing.at[chunk, places[i], pl.ds(0, count)],
            arrived.at[chunk, ctx, pl.ds(0, count)],
            far_out.at[chunk, i], far_in.at[chunk, i],
            device_id=(there + places[i], ch), device_id_type=MESH,
        )

    def near_return(chunk, i):
        return pltpu.make_async_remote_copy(
            results.at[chunk, here + places[i]], returned.at[chunk, place],
            near_back.at[chunk, i], near_home.at[chunk, i],
            device_id=(here + places[i], ch), device_id_type=MESH,
        )

    def far_return(chunk, i):
        if chunk == FIRST:
            src, dst = results.at[chunk, there + places[i]], returned.at[chunk, place]
        else:
            src = results.at[chunk, there + places[i], pl.ds(1, 2)]
            dst = extra.at[chunk, place]
        return pltpu.make_async_remote_copy(
            src, dst, far_back.at[chunk, i], far_home.at[chunk, i],
            device_id=(there + places[i], ch), device_id_type=MESH,
        )

    def own(chunk):
        return pltpu.make_async_copy(
            results.at[chunk, ctx], returned.at[chunk, place], own_sem.at[chunk]
        )

    def prepare(chunk):
        for load in inputs[chunk]:
            load.wait()
        signals = (k_ref[chunk] * v_ref[chunk], f_ref[chunk], g_ref[chunk] * q_ref[chunk])
        for sig, values in enumerate(signals):
            outgoing[chunk, :, sig] = values.T.reshape(PLANES, CHUNK, ROW)
        if chunk == FIRST:

            @pl.when(half == 0)
            def _():
                arrived[chunk, ctx] = outgoing[chunk, place]
        else:
            arrived[chunk, ctx] = outgoing[chunk, place]

    def every(make, chunk):
        return [make(chunk, i) for i in range(NEAR)]

    def part(make, chunk, piece):
        return [make(chunk, i) for i in PIECES[piece]]

    def grant(step):
        for k in range(COLUMN):
            pl.semaphore_signal(
                credit.at[step], inc=1, device_id=(place, lax.rem(ch + k, COLUMN)),
                device_id_type=MESH,
            )

    def granted(step, copies):
        pl.semaphore_wait(credit.at[step], COLUMN)
        start(copies)

    def all_far(make, chunk):
        return [make(chunk, i) for i in range(NEAR + 1)]

    @first_half
    def _():
        prepare(1)
        pl.semaphore_wait(barrier, 2 * NEAR + COLUMN)
        start(all_far(far, 1))
        start(inputs[2] + inputs[3] + loads)
        prepare(0)
        start(every(near, 0))
        prepare(2)
        prepare(3)
        start(every(near, 1))
        for chunk in SECOND:
            arrived[chunk, PLANES:] = jnp.zeros((PLANES, 3, CHUNK, ROW), F32)

    @second_half
    def _():
        prepare(0)
        pl.semaphore_wait(barrier, 2 * NEAR + COLUMN)
        start(all_far(far, 0))
        start(inputs[2] + inputs[3] + loads)
        prepare(1)
        start(every(near, 1))
        prepare(2)
        start(every(near, 2))
        prepare(3)
        start(every(near, 3))
        for chunk in SECOND:
            arrived[chunk, :PLANES, 2] = jnp.zeros((PLANES, CHUNK, ROW), F32)

    for load in loads:
        load.wait()

    def work(chunk):
        for i in range(NEAR):
            near(chunk, i).wait_recv()
        transform(
            arrived.at[chunk], results.at[chunk], outer3, turn_re, turn_im, inner3, back3, wide
        )
        start(every(near_return, chunk))
        own(chunk).start()

    def arrive(make, chunk):
        for i in range(NEAR + 1):
            make(chunk, i).wait_recv()

    def relay(done, follow):
        for before, after in zip(done, follow):
            before.wait_send()
            after.start()

    @first_half
    def _():
        relay(all_far(far, 1), all_far(far, 2))
        start(every(near, 2))
        granted(0, all_far(far, 3))
        start(every(near, 3))
        arrive(far, 0)
        work(0)

    def come(chunk):
        arrive(far, chunk)
        if chunk == 1:
            grant(0)
        if chunk == 2:
            grant(1)

    second_half(lambda: come(1))
    work(1)
    second_half(lambda: start(all_far(far_return, 1)))
    first_half(lambda: granted(1, all_far(far_return, 0)))

    second_half(lambda: come(2))
    work(2)
    second_half(lambda: start(all_far(far_return, 2)))

    second_half(lambda: come(3))
    work(3)
    second_half(lambda: start(all_far(far_return, 3)))

    def finish(chunk):
        for i in range(NEAR):
            near(chunk, i).wait_send()
            near_return(chunk, i).wait()
        own(chunk).wait()

    for chunk in SECOND:
        finish(chunk)

    @first_half
    def _():
        finish(0)
        for copy in all_far(far, 2) + all_far(far, 3) + all_far(far_return, 0):
            copy.wait_send()
        for chunk in SECOND:
            arrive(far_return, chunk)

    @second_half
    def _():
        arrive(far_return, 0)
        for copy in all_far(far, 0):
            copy.wait_send()
        for chunk in SECOND:
            for copy in all_far(far_return, chunk):
                copy.wait_send()


def exchange(query, key, value, taps, cotangent, *consts):
    hbm = pl.BlockSpec(memory_space=pl.ANY)
    signals = pltpu.VMEM((CHUNKS, BLOCKS, 3, CHUNK, ROW), F32)
    near_sem = pltpu.SemaphoreType.DMA((CHUNKS, NEAR))
    far_sem = pltpu.SemaphoreType.DMA((CHUNKS, NEAR + 1))
    return pl.pallas_call(
        exchange_kernel,
        out_shape=[
            jax.ShapeDtypeStruct((CHUNKS, PLANES, 3, CHUNK, ROW), F32),
            jax.ShapeDtypeStruct((CHUNKS, PLANES, 2, CHUNK, ROW), F32),
        ],
        in_specs=[hbm] * 10,
        out_specs=[hbm] * 2,
        scratch_shapes=[
            *[pltpu.VMEM((CHUNKS, ROW, LANES), F32)] * 5,
            pltpu.VMEM((CHUNKS, PLANES, 3, CHUNK, ROW), F32),
            signals,
            signals,
            pltpu.VMEM((3 * SIDE, 6 * ROW), BF16),
            *[pltpu.VMEM(c.shape, c.dtype) for c in consts],
            pltpu.SemaphoreType.DMA((CHUNKS, 5)),
            pltpu.SemaphoreType.DMA((5,)),
            near_sem, near_sem, far_sem, far_sem, near_sem, near_sem, far_sem, far_sem,
            pltpu.SemaphoreType.DMA((CHUNKS,)),
            pltpu.SemaphoreType.REGULAR((2,)),
        ],
        compiler_params=pltpu.CompilerParams(
            collective_id=0, has_side_effects=True, vmem_limit_bytes=60 * 2**20
        ),
        name="exchange",
    )(query, key, value, taps, cotangent, *consts)


def gate_kernel(r_hbm, e_hbm, q_hbm, k_hbm, v_hbm, g_hbm, *rest):
    outs_hbm = rest[:5]
    r_ref, e_ref, q_ref, k_ref, v_ref, g_ref = rest[5:11]
    outs = rest[11:16]
    load_sem, store_sem = rest[16:]
    shared = lax.axis_index("ctx") < PLANES

    def lanes(ref, chunk):
        return ref.at[:, pl.ds(chunk * LANES, LANES)]

    def loads(chunk):
        pairs = [(r_hbm.at[chunk], r_ref.at[chunk])]
        if chunk != FIRST:
            pairs.append((e_hbm.at[chunk], e_ref.at[chunk]))
        for src, dst in ((q_hbm, q_ref), (g_hbm, g_ref), (v_hbm, v_ref), (k_hbm, k_ref)):
            pairs.append((lanes(src, chunk), dst.at[chunk]))
        return [
            pltpu.make_async_copy(src, dst, load_sem.at[chunk, i])
            for i, (src, dst) in enumerate(pairs)
        ]

    def stores(chunk):
        return [
            pltpu.make_async_copy(src.at[chunk], lanes(dst, chunk), store_sem.at[chunk, i])
            for i, (src, dst) in enumerate(zip(outs, outs_hbm))
        ]

    for chunk in range(CHUNKS):
        for load in loads(chunk):
            load.start()
    out, d_query, d_key, d_value, d_taps = outs
    for chunk in range(CHUNKS):
        for load in loads(chunk):
            load.wait()

        def summed(sig):
            mine = r_ref[chunk, :, sig]
            if chunk != FIRST:
                mine = jnp.where(shared, mine + e_ref[chunk, :, sig - 1], mine)
            return mine.reshape(LANES, ROW).T

        convolved = r_ref[chunk, :, 0].reshape(LANES, ROW).T
        out[chunk] = q_ref[chunk] * convolved
        d_query[chunk] = g_ref[chunk] * convolved
        d_mixed = summed(1)
        d_key[chunk] = d_mixed * v_ref[chunk]
        d_value[chunk] = d_mixed * k_ref[chunk]
        d_taps[chunk] = summed(2)
        for store in stores(chunk):
            store.start()
    for chunk in range(CHUNKS):
        for store in stores(chunk):
            store.wait()


def gate(returned, extra, query, key, value, cotangent):
    hbm = pl.BlockSpec(memory_space=pl.ANY)
    return pl.pallas_call(
        gate_kernel,
        out_shape=[jax.ShapeDtypeStruct(query.shape, F32)] * 5,
        in_specs=[hbm] * 6,
        out_specs=[hbm] * 5,
        scratch_shapes=[
            pltpu.VMEM(returned.shape, F32),
            pltpu.VMEM(extra.shape, F32),
            *[pltpu.VMEM((CHUNKS, ROW, LANES), F32)] * 9,
            pltpu.SemaphoreType.DMA((CHUNKS, 6)),
            pltpu.SemaphoreType.DMA((CHUNKS, 5)),
        ],
        compiler_params=pltpu.CompilerParams(vmem_limit_bytes=60 * 2**20),
        name="gate",
    )(returned, extra, query, key, value, cotangent)


def shards(query, key, value, taps, cotangent):
    consts = [jnp.asarray(c) for c in tables()]
    returned, extra = exchange(query, key, value, taps, cotangent, *consts)
    return tuple(gate(returned, extra, query, key, value, cotangent))


def solution(mesh):
    placed = P("ctx", "ch")
    return jax.shard_map(
        shards,
        mesh=mesh,
        in_specs=(placed,) * 5,
        out_specs=(placed,) * 5,
        check_vma=False,
    )
```

```python
import functools
import math

import jax
import jax.numpy as jnp
import ml_dtypes
import numpy as np
from jax import lax
from jax.experimental import pallas as pl
from jax.experimental.pallas import tpu as pltpu
from jax.sharding import PartitionSpec as P

MESH = pl.DeviceIdType.MESH
BF16 = jnp.bfloat16
F32 = jnp.float32

BLOCKS = 32
PLANES = 16
ROW = 256
CHUNK = 8
CHUNKS = 4
LANES = PLANES * CHUNK
FIRST = 0
SECOND = tuple(c for c in range(CHUNKS) if c != FIRST)
SIDE = BLOCKS * CHUNK
PADDED = 2 * BLOCKS * ROW

OFFSETS = (
    (2, 2), (1, 2), (2, 1), (2, 3), (3, 2), (0, 2), (1, 1), (1, 3), (2, 0), (3, 1), (3, 3), (0, 1), (0, 3), (1, 0), (3, 0), (0, 0),
)
NEAR = len(OFFSETS) - 1
COLUMN = 8
PIECES = (tuple(range(8)), tuple(range(8, NEAR + 1)))


def split_np(values):
    high = values.astype(ml_dtypes.bfloat16)
    low = (values - high.astype(np.float64)).astype(ml_dtypes.bfloat16)
    return high, low


@functools.lru_cache(maxsize=None)
def tables():
    two_pi = 2.0 * math.pi
    half = np.arange(BLOCKS) + 0.5
    block = np.arange(BLOCKS)
    row = np.arange(ROW)
    eye = np.eye(CHUNK)
    psi = two_pi * np.outer(half, block) / (2 * BLOCKS)
    outer = np.concatenate([np.kron(np.cos(psi), eye), np.kron(-np.sin(psi), eye)], axis=0)
    high, low = split_np(outer)
    outer3 = np.concatenate([high, low, high], axis=1)
    theta = two_pi * np.outer(half, row) / PADDED
    turn_re = np.repeat(np.cos(theta), CHUNK, axis=0).astype(np.float32)
    turn_im = np.repeat(-np.sin(theta), CHUNK, axis=0).astype(np.float32)
    phi = two_pi * (np.outer(row, row) % ROW) / ROW
    inner = np.block([[np.cos(phi), -np.sin(phi)], [np.sin(phi), np.cos(phi)]])
    high, low = split_np(inner)
    inner3 = np.concatenate([high, high, low], axis=0)
    back = np.concatenate([np.kron(np.cos(psi.T), eye), np.kron(np.sin(psi.T), eye)], axis=1)
    high, low = split_np(back * (2.0 / PADDED))
    back3 = np.concatenate([high, low, high], axis=1)
    return outer3, turn_re, turn_im, inner3, back3


def halves(values):
    high = values.astype(BF16)
    return high, (values - high.astype(F32)).astype(BF16)


def transform(arrived, results, outer3, turn_re, turn_im, inner3, back3, wide):
    t_re = turn_re[...]
    t_im = turn_im[...]
    for sig in range(3):
        high, low = halves(arrived[:, sig].reshape(SIDE, ROW))
        mixed = jnp.dot(
            outer3[...], jnp.concatenate([high, high, low], axis=0), preferred_element_type=F32
        )
        z_re, z_im = mixed[:SIDE], mixed[SIDE:]
        rows = pl.ds(sig * SIDE, SIDE)
        high, low = halves(z_re * t_re - z_im * t_im)
        wide[rows, 0 * ROW : 1 * ROW] = high
        wide[rows, 2 * ROW : 3 * ROW] = low
        wide[rows, 4 * ROW : 5 * ROW] = high
        high, low = halves(z_re * t_im + z_im * t_re)
        wide[rows, 1 * ROW : 2 * ROW] = high
        wide[rows, 3 * ROW : 4 * ROW] = low
        wide[rows, 5 * ROW : 6 * ROW] = high
    spec = jnp.dot(wide[...], inner3[...], preferred_element_type=F32)
    m_re, m_im = spec[:SIDE, :ROW], spec[:SIDE, ROW:]
    h_re, h_im = spec[SIDE : 2 * SIDE, :ROW], spec[SIDE : 2 * SIDE, ROW:]
    u_re, u_im = spec[2 * SIDE :, :ROW], spec[2 * SIDE :, ROW:]
    products = (
        (m_re * h_re - m_im * h_im, -(m_re * h_im + m_im * h_re)),
        (h_re * u_re + h_im * u_im, h_im * u_re - h_re * u_im),
        (m_re * u_re + m_im * u_im, m_im * u_re - m_re * u_im),
    )
    for sig, (p_re, p_im) in enumerate(products):
        rows = pl.ds(sig * SIDE, SIDE)
        high, low = halves(p_re)
        wide[rows, 0 * ROW : 1 * ROW] = high
        wide[rows, 2 * ROW : 3 * ROW] = low
        wide[rows, 4 * ROW : 5 * ROW] = high
        high, low = halves(p_im)
        wide[rows, 1 * ROW : 2 * ROW] = high
        wide[rows, 3 * ROW : 4 * ROW] = low
        wide[rows, 5 * ROW : 6 * ROW] = high
    inv = jnp.dot(wide[...], inner3[...], preferred_element_type=F32)
    for sig in range(3):
        v_re = inv[sig * SIDE : (sig + 1) * SIDE, :ROW]
        v_im = inv[sig * SIDE : (sig + 1) * SIDE, ROW:]
        re_high, re_low = halves(v_re * t_re - v_im * t_im)
        im_high, im_low = halves(v_re * t_im + v_im * t_re)
        stacked = jnp.concatenate([re_high, im_high, re_high, im_high, re_low, im_low], axis=0)
        out = jnp.dot(back3[...], stacked, preferred_element_type=F32)
        results[:, sig] = out.reshape(BLOCKS, CHUNK, ROW)


def exchange_kernel(
    q_hbm, k_hbm, v_hbm, f_hbm, g_hbm, outer_hbm, re_hbm, im_hbm, inner_hbm, back_hbm,
    returned, extra,
    q_ref, k_ref, v_ref, f_ref, g_ref, outgoing, arrived, results,
    wide, outer3, turn_re, turn_im, inner3, back3,
    input_sem, table_sem, near_out, near_in, far_out, far_in,
    near_back, near_home, far_back, far_home, own_sem, credit,
):
    ctx = lax.axis_index("ctx")
    ch = lax.axis_index("ch")
    half = ctx // PLANES
    place = lax.rem(ctx, PLANES)
    x = place // 4
    y = lax.rem(place, 4)
    places = [lax.rem(x + dx, 4) * 4 + lax.rem(y + dy, 4) for dx, dy in OFFSETS]
    here = half * PLANES
    there = PLANES - here

    pairs = (
        (k_hbm, k_ref), (v_hbm, v_ref), (f_hbm, f_ref), (g_hbm, g_ref), (q_hbm, q_ref)
    )
    inputs = [
        [
            pltpu.make_async_copy(
                src.at[:, pl.ds(chunk * LANES, LANES)], dst.at[chunk], input_sem.at[chunk, i]
            )
            for i, (src, dst) in enumerate(pairs)
        ]
        for chunk in range(CHUNKS)
    ]
    def start(copies):
        for copy in copies:
            copy.start()

    def first_half(body):
        pl.when(half == 0)(body)

    def second_half(body):
        pl.when(half == 1)(body)

    first_half(lambda: start(inputs[1]))
    second_half(lambda: start(inputs[0]))

    barrier = pltpu.get_barrier_semaphore()
    for i in range(NEAR + 1):
        if i < NEAR:
            pl.semaphore_signal(
                barrier, inc=1, device_id=(here + places[i], ch), device_id_type=MESH
            )
        pl.semaphore_signal(
            barrier, inc=1, device_id=(there + places[i], ch), device_id_type=MESH
        )
    for k in range(1, COLUMN):
        pl.semaphore_signal(
            barrier, inc=1, device_id=(there + place, lax.rem(ch + k, COLUMN)),
            device_id_type=MESH,
        )

    loads = [
        pltpu.make_async_copy(src, dst, table_sem.at[i])
        for i, (src, dst) in enumerate(
            (
                (outer_hbm, outer3), (re_hbm, turn_re), (im_hbm, turn_im),
                (inner_hbm, inner3), (back_hbm, back3),
            )
        )
    ]
    first_half(lambda: start(inputs[0]))
    second_half(lambda: start(inputs[1]))

    def near(chunk, i):
        return pltpu.make_async_remote_copy(
            outgoing.at[chunk, places[i]], arrived.at[chunk, ctx],
            near_out.at[chunk, i], near_in.at[chunk, i],
            device_id=(here + places[i], ch), device_id_type=MESH,
        )

    def far(chunk, i):
        count = 3 if chunk == FIRST else 2
        return pltpu.make_async_remote_copy(
            outgoing.at[chunk, places[i], pl.ds(0, count)],
            arrived.at[chunk, ctx, pl.ds(0, count)],
            far_out.at[chunk, i], far_in.at[chunk, i],
            device_id=(there + places[i], ch), device_id_type=MESH,
        )

    def near_return(chunk, i):
        return pltpu.make_async_remote_copy(
            results.at[chunk, here + places[i]], returned.at[chunk, place],
            near_back.at[chunk, i], near_home.at[chunk, i],
            device_id=(here + places[i], ch), device_id_type=MESH,
        )

    def far_return(chunk, i):
        if chunk == FIRST:
            src, dst = results.at[chunk, there + places[i]], returned.at[chunk, place]
        else:
            src = results.at[chunk, there + places[i], pl.ds(1, 2)]
            dst = extra.at[chunk, place]
        return pltpu.make_async_remote_copy(
            src, dst, far_back.at[chunk, i], far_home.at[chunk, i],
            device_id=(there + places[i], ch), device_id_type=MESH,
        )

    def own(chunk):
        return pltpu.make_async_copy(
            results.at[chunk, ctx], returned.at[chunk, place], own_sem.at[chunk]
        )

    def prepare(chunk):
        for load in inputs[chunk]:
            load.wait()
        signals = (k_ref[chunk] * v_ref[chunk], f_ref[chunk], g_ref[chunk] * q_ref[chunk])
        for sig, values in enumerate(signals):
            outgoing[chunk, :, sig] = values.T.reshape(PLANES, CHUNK, ROW)
        if chunk == FIRST:

            @pl.when(half == 0)
            def _():
                arrived[chunk, ctx] = outgoing[chunk, place]
        else:
            arrived[chunk, ctx] = outgoing[chunk, place]

    def every(make, chunk):
        return [make(chunk, i) for i in range(NEAR)]

    def part(make, chunk, piece):
        return [make(chunk, i) for i in PIECES[piece]]

    def grant(step):
        for k in range(COLUMN):
            pl.semaphore_signal(
                credit.at[step], inc=1, device_id=(place, lax.rem(ch + k, COLUMN)),
                device_id_type=MESH,
            )

    def granted(step, copies):
        pl.semaphore_wait(credit.at[step], COLUMN)
        start(copies)

    def all_far(make, chunk):
        return [make(chunk, i) for i in range(NEAR + 1)]

    @first_half
    def _():
        prepare(1)
        pl.semaphore_wait(barrier, 2 * NEAR + COLUMN)
        start(all_far(far, 1))
        start(inputs[2] + inputs[3] + loads)
        prepare(0)
        start(every(near, 0))
        prepare(2)
        prepare(3)
        start(every(near, 1))
        for chunk in SECOND:
            arrived[chunk, PLANES:] = jnp.zeros((PLANES, 3, CHUNK, ROW), F32)

    @second_half
    def _():
        prepare(0)
        pl.semaphore_wait(barrier, 2 * NEAR + COLUMN)
        start(all_far(far, 0))
        start(inputs[2] + inputs[3] + loads)
        prepare(1)
        start(every(near, 1))
        prepare(2)
        start(every(near, 2))
        prepare(3)
        start(every(near, 3))
        for chunk in SECOND:
            arrived[chunk, :PLANES, 2] = jnp.zeros((PLANES, CHUNK, ROW), F32)

    for load in loads:
        load.wait()

    def work(chunk):
        for i in range(NEAR):
            near(chunk, i).wait_recv()
        transform(
            arrived.at[chunk], results.at[chunk], outer3, turn_re, turn_im, inner3, back3, wide
        )
        start(every(near_return, chunk))
        own(chunk).start()

    def arrive(make, chunk):
        for i in range(NEAR + 1):
            make(chunk, i).wait_recv()

    def relay(done, follow):
        for before, after in zip(done, follow):
            before.wait_send()
            after.start()

    @first_half
    def _():
        relay(all_far(far, 1), all_far(far, 2))
        start(every(near, 2))
        granted(0, all_far(far, 3))
        start(every(near, 3))
        arrive(far, 0)
        work(0)

    def come(chunk):
        arrive(far, chunk)
        if chunk == 1:
            grant(0)
        if chunk == 2:
            grant(1)

    second_half(lambda: come(1))
    work(1)
    second_half(lambda: start(all_far(far_return, 1)))
    first_half(lambda: granted(1, all_far(far_return, 0)))

    second_half(lambda: come(2))
    work(2)
    second_half(lambda: start(all_far(far_return, 2)))

    second_half(lambda: come(3))
    work(3)
    second_half(lambda: start(all_far(far_return, 3)))

    def finish(chunk):
        for i in range(NEAR):
            near(chunk, i).wait_send()
            near_return(chunk, i).wait()
        own(chunk).wait()

    for chunk in SECOND:
        finish(chunk)

    @first_half
    def _():
        finish(0)
        for copy in all_far(far, 2) + all_far(far, 3) + all_far(far_return, 0):
            copy.wait_send()
        for chunk in SECOND:
            arrive(far_return, chunk)

    @second_half
    def _():
        arrive(far_return, 0)
        for copy in all_far(far, 0):
            copy.wait_send()
        for chunk in SECOND:
            for copy in all_far(far_return, chunk):
                copy.wait_send()


def exchange(query, key, value, taps, cotangent, *consts):
    hbm = pl.BlockSpec(memory_space=pl.ANY)
    signals = pltpu.VMEM((CHUNKS, BLOCKS, 3, CHUNK, ROW), F32)
    near_sem = pltpu.SemaphoreType.DMA((CHUNKS, NEAR))
    far_sem = pltpu.SemaphoreType.DMA((CHUNKS, NEAR + 1))
    return pl.pallas_call(
        exchange_kernel,
        out_shape=[
            jax.ShapeDtypeStruct((CHUNKS, PLANES, 3, CHUNK, ROW), F32),
            jax.ShapeDtypeStruct((CHUNKS, PLANES, 2, CHUNK, ROW), F32),
        ],
        in_specs=[hbm] * 10,
        out_specs=[hbm] * 2,
        scratch_shapes=[
            *[pltpu.VMEM((CHUNKS, ROW, LANES), F32)] * 5,
            pltpu.VMEM((CHUNKS, PLANES, 3, CHUNK, ROW), F32),
            signals,
            signals,
            pltpu.VMEM((3 * SIDE, 6 * ROW), BF16),
            *[pltpu.VMEM(c.shape, c.dtype) for c in consts],
            pltpu.SemaphoreType.DMA((CHUNKS, 5)),
            pltpu.SemaphoreType.DMA((5,)),
            near_sem, near_sem, far_sem, far_sem, near_sem, near_sem, far_sem, far_sem,
            pltpu.SemaphoreType.DMA((CHUNKS,)),
            pltpu.SemaphoreType.REGULAR((2,)),
        ],
        compiler_params=pltpu.CompilerParams(
            collective_id=0, has_side_effects=True, vmem_limit_bytes=60 * 2**20
        ),
        name="exchange",
    )(query, key, value, taps, cotangent, *consts)


def gate_kernel(r_hbm, e_hbm, q_hbm, k_hbm, v_hbm, g_hbm, *rest):
    outs_hbm = rest[:5]
    r_ref, e_ref, q_ref, k_ref, v_ref, g_ref = rest[5:11]
    outs = rest[11:16]
    load_sem, store_sem = rest[16:]
    shared = lax.axis_index("ctx") < PLANES

    def lanes(ref, chunk):
        return ref.at[:, pl.ds(chunk * LANES, LANES)]

    def loads(chunk):
        pairs = [(r_hbm.at[chunk], r_ref.at[chunk])]
        if chunk != FIRST:
            pairs.append((e_hbm.at[chunk], e_ref.at[chunk]))
        for src, dst in ((q_hbm, q_ref), (g_hbm, g_ref), (v_hbm, v_ref), (k_hbm, k_ref)):
            pairs.append((lanes(src, chunk), dst.at[chunk]))
        return [
            pltpu.make_async_copy(src, dst, load_sem.at[chunk, i])
            for i, (src, dst) in enumerate(pairs)
        ]

    def stores(chunk):
        return [
            pltpu.make_async_copy(src.at[chunk], lanes(dst, chunk), store_sem.at[chunk, i])
            for i, (src, dst) in enumerate(zip(outs, outs_hbm))
        ]

    for chunk in range(CHUNKS):
        for load in loads(chunk):
            load.start()
    out, d_query, d_key, d_value, d_taps = outs
    for chunk in range(CHUNKS):
        for load in loads(chunk):
            load.wait()

        def summed(sig):
            mine = r_ref[chunk, :, sig]
            if chunk != FIRST:
                mine = jnp.where(shared, mine + e_ref[chunk, :, sig - 1], mine)
            return mine.reshape(LANES, ROW).T

        convolved = r_ref[chunk, :, 0].reshape(LANES, ROW).T
        out[chunk] = q_ref[chunk] * convolved
        d_query[chunk] = g_ref[chunk] * convolved
        d_mixed = summed(1)
        d_key[chunk] = d_mixed * v_ref[chunk]
        d_value[chunk] = d_mixed * k_ref[chunk]
        d_taps[chunk] = summed(2)
        for store in stores(chunk):
            store.start()
    for chunk in range(CHUNKS):
        for store in stores(chunk):
            store.wait()


def gate(returned, extra, query, key, value, cotangent):
    hbm = pl.BlockSpec(memory_space=pl.ANY)
    return pl.pallas_call(
        gate_kernel,
        out_shape=[jax.ShapeDtypeStruct(query.shape, F32)] * 5,
        in_specs=[hbm] * 6,
        out_specs=[hbm] * 5,
        scratch_shapes=[
            pltpu.VMEM(returned.shape, F32),
            pltpu.VMEM(extra.shape, F32),
            *[pltpu.VMEM((CHUNKS, ROW, LANES), F32)] * 9,
            pltpu.SemaphoreType.DMA((CHUNKS, 6)),
            pltpu.SemaphoreType.DMA((CHUNKS, 5)),
        ],
        compiler_params=pltpu.CompilerParams(vmem_limit_bytes=60 * 2**20),
        name="gate",
    )(returned, extra, query, key, value, cotangent)


def shards(query, key, value, taps, cotangent):
    consts = [jnp.asarray(c) for c in tables()]
    returned, extra = exchange(query, key, value, taps, cotangent, *consts)
    return tuple(gate(returned, extra, query, key, value, cotangent))


def solution(mesh):
    placed = P("ctx", "ch")
    return jax.shard_map(
        shards,
        mesh=mesh,
        in_specs=(placed,) * 5,
        out_specs=(placed,) * 5,
        check_vma=False,
    )
```
